32 devices in a mesh: row: 4 (over x, core), col: 8 (over z, y).
Axes of the slice: x: 2, y: 2, z: 4, core: 2. Of those that a mesh axis runs over, the one named last changes fastest.
Arguments:
- features: bfloat16 [4096, 256], P(('row', 'col')), may hold values from -6 to 6
- blocks: bfloat16 [32, 32, 128, 128], P('row', 'col'), may hold values from -0.09375 to 0.09375
- block_col: int32 [32, 32], P('row', 'col'), may hold values from 0 to 3
- row_count: int32 [32, 8], P('row', 'col'), may hold values from 0 to 4, as said below
- weight: bfloat16 [256, 256], replicated, may hold values from -0.375 to 0.375
- out_bias: float32 [256], replicated, may hold values from -4 to 4
Outputs:
- layer_out: bfloat16 [4096, 256], P(('row', 'col'))
The draws below stay inside these ranges and needn't reach their ends.
Inputs may be any that keep to these rules, and one draw needn't show every extreme that they name: row_count[i, j] is how many of the 4 slots of block row i in column group j are in use; the others are ignored.
All inputs are finite; a program needn't handle non-finite values.
Results may differ from the reference program's by a relative error of at most 0.018.
Values may be sent and summed in bfloat16 or wider, within the bound.
A program may use at most 64 MiB of HBM per device.

```python
import jax
import jax.numpy as jnp
from jax import lax

F = 256
BS = 128
KR = 4
RB = 8
CB = 4
BROWS = 32
NODES = 4096
N_ROW = 4
N_COL = 8


def draw_row_count(key, part):
    subkeys = jax.random.split(key, 5)
    base_count = jax.random.randint(subkeys[0], (BROWS, N_COL), 0, KR // 2 + 1)
    full_rows = jax.random.randint(subkeys[1], (BROWS, N_COL), 0, 8) == 0
    heavy_dev = jax.random.randint(subkeys[2], (N_ROW, N_COL), 0, 4) == 0
    heavy_rows = jnp.repeat(heavy_dev, RB, axis=0)
    counts = jnp.where(full_rows | heavy_rows, KR, base_count)
    pick_row = jax.random.randint(subkeys[3], (), 0, BROWS)
    pick_col = jax.random.randint(subkeys[4], (), 0, N_COL)
    return counts.at[pick_row, pick_col].set(KR).astype(jnp.int32)


def with_ends(values, own_key, low, top_value):
    longest = values.shape.index(max(values.shape))
    spots = []
    for shift in (0, 1):
        where = [jax.random.randint(jax.random.fold_in(own_key, axis), (), 0, length) for axis, length in enumerate(values.shape)]
        where[longest] = (where[longest] + shift) % values.shape[longest]
        spots.append(tuple(where))
    return values.at[spots[0]].set(low).at[spots[1]].set(top_value)


def level_of(own_key, shape, pieces, low, top_value):
    gain, own = 1.0, jax.random.fold_in(own_key, 6)
    for position, shards_of in pieces:
        steps = jnp.exp(jax.random.uniform(jax.random.fold_in(own, position), (shards_of,), jnp.float32, low / len(pieces), top_value / len(pieces)))
        gain = gain * jnp.repeat(steps, shape[position] // shards_of).reshape([-1 if axis == position else 1 for axis in range(len(shape))])
    return gain


def gaussian(key, dims, deviation, most, cuts=(), kind=jnp.bfloat16):
    level = level_of(key, dims, cuts, -0.22, 0.18) if cuts else 1.0
    values = jax.random.normal(key, dims, jnp.float32) * deviation * level
    return jnp.minimum(jnp.maximum(values, -most), most).astype(kind)


def setup_inputs(seed: int = 0) -> dict:
    arg_keys = jax.random.split(jax.random.key(seed), 7)
    features = gaussian(arg_keys[0], (NODES, F), 1.0, 6.0, ((0, 32),))
    blocks = gaussian(arg_keys[1], (BROWS, N_COL * KR, BS, BS), (BS * KR * N_COL) ** -0.5, 0.09375, ((0, 4), (1, 8)))
    block_col = with_ends(jax.random.randint(arg_keys[2], (BROWS, N_COL * KR), 0, CB), jax.random.fold_in(arg_keys[2], 1), 0, CB - 1).astype(jnp.int32)
    row_count = draw_row_count(jax.random.fold_in(arg_keys[6], 71), 0)
    weight = gaussian(arg_keys[4], (F, F), F ** -0.5, 0.375)
    out_bias = gaussian(arg_keys[5], (F,), 1.0, 4.0, (), jnp.float32)
    return dict(features=features, blocks=blocks, block_col=block_col, row_count=row_count, weight=weight, out_bias=out_bias)


def local_terms(blocks, block_col, counts, stripe):
    slot_ids = jnp.arange(block_col.shape[1], dtype=jnp.int32)[None, :]
    live_slots = (slot_ids < counts).astype(jnp.float32)
    picked = stripe[block_col].astype(jnp.float32) * live_slots[:, :, None, None]
    term_rows = jnp.einsum("ikab,ikbf->iaf", blocks.astype(jnp.float32), picked, precision=lax.Precision.HIGHEST)
    return term_rows.reshape(-1, stripe.shape[2])


def reference(features, blocks, block_col, row_count, weight, out_bias):
    feat_width = features.shape[1]
    block_size = blocks.shape[2]
    per_device = features.shape[0] // (N_ROW * N_COL)
    band_rows = blocks.shape[0] // N_ROW
    slot_count = blocks.shape[1] // N_COL
    grid_feat = features.reshape(N_ROW, N_COL, per_device, feat_width)
    stripes = jnp.transpose(grid_feat, (1, 0, 2, 3)).reshape(N_COL, -1, block_size, feat_width)
    grid_blocks = blocks.reshape(N_ROW, band_rows, N_COL, slot_count, block_size, block_size)
    grid_cols = block_col.reshape(N_ROW, band_rows, N_COL, slot_count)
    grid_counts = row_count.reshape(N_ROW, band_rows, N_COL)

    def one_band(packed):
        band_blocks, band_cols, band_counts = packed
        moved_blocks = jnp.moveaxis(band_blocks, 1, 0)
        moved_cols = jnp.moveaxis(band_cols, 1, 0)
        moved_counts = jnp.moveaxis(band_counts, 1, 0)

        def add_group(total, items):
            grp_blocks, grp_cols, grp_counts, grp_stripe = items
            term_rows = local_terms(grp_blocks, grp_cols, grp_counts[:, None], grp_stripe)
            rounded = lax.optimization_barrier(term_rows.astype(jnp.bfloat16))
            return total + rounded.astype(jnp.float32), None

        start_total = jnp.zeros((band_rows * block_size, feat_width), jnp.float32)
        total, _ = lax.scan(add_group, start_total, (moved_blocks, moved_cols, moved_counts, stripes))
        return total

    aggregate = lax.map(one_band, (grid_blocks, grid_cols, grid_counts)).reshape(-1, feat_width)
    hidden = jnp.dot(aggregate.astype(jnp.bfloat16), weight, preferred_element_type=jnp.float32) + out_bias
    return jnp.maximum(hidden, 0.0).astype(jnp.bfloat16)
```

```python
import functools

import jax
import jax.numpy as jnp
from jax import lax
from jax.experimental import pallas as pl
from jax.experimental.pallas import tpu as pltpu
from jax.sharding import PartitionSpec as P

MESH = pl.DeviceIdType.MESH
HALVES = 2
INNER = 2


def layer_kernel(
    n_row, n_out, bs,
    feat_hbm, blocks_hbm, col_hbm, count_hbm, weight_hbm, bias_hbm, out_ref,
    feat, blocks, cols, counts, weight, bias, stripe, dense, terms, pair_in, pair_out, owner_in,
    load_sem, ag_send, ag_recv, pair_send, pair_recv, owner_send, owner_recv,
):
    row = lax.axis_index("row")
    col = lax.axis_index("col")
    outer, inner = col // INNER, col % INNER
    partner = outer * INNER + 1 - inner
    width = stripe.shape[2]
    slots = blocks.shape[1]

    def load(index, src, dst):
        copy = pltpu.make_async_copy(src, dst, load_sem.at[index])
        copy.start()
        return copy

    barrier = pltpu.get_barrier_semaphore()
    for shift in range(1, n_row):
        pl.semaphore_signal(barrier, inc=1, device_id=(lax.rem(row + shift, n_row), col), device_id_type=MESH)
    pl.semaphore_signal(barrier, inc=1, device_id=(row, partner), device_id_type=MESH)
    for shift in range(1, n_out):
        pl.semaphore_signal(
            barrier, inc=1, device_id=(row, lax.rem(outer + shift, n_out) * INNER + inner), device_id_type=MESH
        )

    feat_load = load(0, feat_hbm, feat)
    weight_load = load(1, weight_hbm, weight)
    col_load = load(2, col_hbm, cols)
    count_load = load(3, count_hbm, counts)
    block_load = load(4, blocks_hbm, blocks)
    bias_load = load(5, bias_hbm, bias)

    def owner_of(i):
        down = n_out - 1 - i
        down = down - (down <= outer).astype(jnp.int32)
        up = i + (i >= outer).astype(jnp.int32)
        low = (outer < n_out // 2).astype(jnp.int32)
        last = jnp.where(i == n_out - 1, 1, 0)
        return last * outer + (1 - last) * (low * down + (1 - low) * up)

    feat_load.wait()
    weight_load.wait()
    own_rows = pl.ds(pl.multiple_of(row * bs, bs), bs)
    product = jnp.dot(feat[...], weight[...], preferred_element_type=jnp.float32).astype(jnp.bfloat16)
    for half in range(HALVES):
        stripe[half, own_rows, :] = product[:, half * width:(half + 1) * width]

    pl.semaphore_wait(barrier, n_row - 1 + 1 + n_out - 1)

    gathers = []
    for half in range(HALVES):
        for shift in range(1, n_row):
            copy = pltpu.make_async_remote_copy(
                src_ref=stripe.at[half, own_rows, :],
                dst_ref=stripe.at[half, own_rows, :],
                send_sem=ag_send.at[half, shift - 1],
                recv_sem=ag_recv.at[half, shift - 1],
                device_id=(lax.rem(row + shift, n_row), col),
                device_id_type=MESH,
            )
            copy.start()
            gathers.append(copy)

    col_load.wait()
    count_load.wait()
    block_load.wait()

    def build(slot, carry):
        group, i = slot // n_out, slot % n_out
        target = owner_of(i) * INNER + (1 - group) * (1 - inner) + group * inner
        rows = pl.ds(pl.multiple_of(slot * bs, bs), bs)
        count = counts[0, target]
        parts = [blocks[target, k].astype(jnp.float32) for k in range(slots)]
        for j in range(n_row):
            total = None
            for k in range(slots):
                live = jnp.logical_and(cols[k, target] == j, k < count)
                piece = parts[k] * jnp.where(live, 1.0, 0.0).astype(jnp.float32)
                total = piece if total is None else total + piece
            dense[rows, j * bs:(j + 1) * bs] = total.astype(jnp.bfloat16)
        return carry

    lax.fori_loop(0, INNER * n_out, build, 0)

    step = 4 if n_out % 4 == 0 else 1

    def multiply(half, group):
        def some(index, carry):
            first = group * n_out + index * step
            rows = pl.ds(pl.multiple_of(first * bs, bs), step * bs)
            value = jnp.dot(dense[rows, :], stripe[half], preferred_element_type=jnp.float32)
            terms[half, rows, :] = value.astype(jnp.bfloat16)
            return carry

        if n_out == step:
            some(0, 0)
        else:
            lax.fori_loop(0, n_out // step, some, 0)

    pairs = []
    for half in range(HALVES):
        for shift in range(1, n_row):
            gathers[half * (n_row - 1) + shift - 1].wait_recv()
        multiply(half, 0)
        for i in range(n_out):
            copy = pltpu.make_async_remote_copy(
                src_ref=terms.at[half, pl.ds(i * bs, bs), :],
                dst_ref=pair_in.at[half, i],
                send_sem=pair_send.at[half, i],
                recv_sem=pair_recv.at[half, i],
                device_id=(row, partner),
                device_id_type=MESH,
            )
            copy.start()
            pairs.append(copy)
        multiply(half, 1)

    owners, mine = [], []
    for half in range(HALVES):
        for i in range(n_out):
            pairs[half * n_out + i].wait_recv()
            first = (n_out + i) * bs
            total = terms[half, first:first + bs, :].astype(jnp.float32) + pair_in[half, i].astype(jnp.float32)
            if i == n_out - 1:
                mine.append(total)
                continue
            pair_out[half, i] = total.astype(jnp.bfloat16)
            target = owner_of(i)
            shift = lax.rem(target - outer + n_out, n_out) - 1
            copy = pltpu.make_async_remote_copy(
                src_ref=pair_out.at[half, i],
                dst_ref=owner_in.at[half, shift],
                send_sem=owner_send.at[half, i],
                recv_sem=owner_recv.at[half, shift],
                device_id=(row, target * INNER + inner),
                device_id_type=MESH,
            )
            copy.start()
            owners.append(copy)

    bias_load.wait()
    for half in range(HALVES):
        total = mine[half]
        for shift in range(n_out - 1):
            pltpu.make_async_remote_copy(
                src_ref=pair_out.at[half, 0],
                dst_ref=owner_in.at[half, shift],
                send_sem=owner_send.at[half, 0],
                recv_sem=owner_recv.at[half, shift],
                device_id=(row, partner),
                device_id_type=MESH,
            ).wait_recv()
            total = total + owner_in[half, shift].astype(jnp.float32)
        span = slice(half * width, (half + 1) * width)
        out_ref[:, span] = jnp.maximum(total + bias[:, span], 0.0).astype(jnp.bfloat16)

    for copy in gathers + pairs + owners:
        copy.wait_send()


def local(n_row, n_col, features, blocks, block_col, row_count, weight, out_bias):
    bs, feat_width = blocks.shape[2], features.shape[1]
    n_out = n_col // INNER
    width = feat_width // HALVES
    bf16 = jnp.bfloat16
    return pl.pallas_call(
        functools.partial(layer_kernel, n_row, n_out, bs),
        out_shape=jax.ShapeDtypeStruct(features.shape, bf16),
        in_specs=[pl.BlockSpec(memory_space=pltpu.HBM)] * 6,
        out_specs=pl.BlockSpec(memory_space=pltpu.VMEM),
        scratch_shapes=[
            pltpu.VMEM(features.shape, bf16),
            pltpu.VMEM(blocks.shape, bf16),
            pltpu.SMEM(block_col.shape[::-1], jnp.int32),
            pltpu.SMEM(row_count.shape[::-1], jnp.int32),
            pltpu.VMEM(weight.shape, bf16),
            pltpu.VMEM((1, feat_width), jnp.float32),
            pltpu.VMEM((HALVES, n_row * bs, width), bf16),
            pltpu.VMEM((n_col * bs, n_row * bs), bf16),
            pltpu.VMEM((HALVES, n_col * bs, width), bf16),
            pltpu.VMEM((HALVES, n_out, bs, width), bf16),
            pltpu.VMEM((HALVES, n_out - 1, bs, width), bf16),
            pltpu.VMEM((HALVES, n_out - 1, bs, width), bf16),
            pltpu.SemaphoreType.DMA((6,)),
            pltpu.SemaphoreType.DMA((HALVES, n_row - 1)),
            pltpu.SemaphoreType.DMA((HALVES, n_row - 1)),
            pltpu.SemaphoreType.DMA((HALVES, n_out)),
            pltpu.SemaphoreType.DMA((HALVES, n_out)),
            pltpu.SemaphoreType.DMA((HALVES, n_out - 1)),
            pltpu.SemaphoreType.DMA((HALVES, n_out - 1)),
        ],
        compiler_params=pltpu.CompilerParams(
            collective_id=0, has_side_effects=True, vmem_limit_bytes=52 * 1024 * 1024
        ),
    )(features, blocks, block_col.T, row_count.T, weight, out_bias.reshape(1, feat_width))


def solution(mesh):
    return jax.shard_map(
        functools.partial(local, mesh.shape["row"], mesh.shape["col"]),
        mesh=mesh,
        in_specs=(
            P(("row", "col"), None),
            P("row", "col", None, None),
            P("row", "col"),
            P("row", "col"),
            P(),
            P(),
        ),
        out_specs=P(("row", "col"), None),
        check_vma=False,
    )
```

```python
import functools

import jax
import jax.numpy as jnp
from jax import lax
from jax.experimental import pallas as pl
from jax.experimental.pallas import tpu as pltpu
from jax.sharding import PartitionSpec as P

MESH = pl.DeviceIdType.MESH
HALVES = 2
INNER = 2


def layer_kernel(
    n_row, n_out, bs,
    feat_hbm, blocks_hbm, col_hbm, count_hbm, weight_hbm, bias_hbm, out_ref,
    blocks, cols, counts, weight, bias, stripe, dense, terms, pair_in, pair_out, owner_in,
    load_sem, ag_send, ag_recv, pair_send, pair_recv, owner_send, owner_recv,
):
    row = lax.axis_index("row")
    col = lax.axis_index("col")
    outer, inner = col // INNER, col % INNER
    partner = outer * INNER + 1 - inner
    width = stripe.shape[2]
    slots = blocks.shape[1]

    def load(index, src, dst):
        copy = pltpu.make_async_copy(src, dst, load_sem.at[index])
        copy.start()
        return copy

    barrier = pltpu.get_barrier_semaphore()
    for shift in range(1, n_row):
        pl.semaphore_signal(barrier, inc=1, device_id=(lax.rem(row + shift, n_row), col), device_id_type=MESH)
    pl.semaphore_signal(barrier, inc=1, device_id=(row, partner), device_id_type=MESH)
    for shift in range(1, n_out):
        pl.semaphore_signal(
            barrier, inc=1, device_id=(row, lax.rem(outer + shift, n_out) * INNER + inner), device_id_type=MESH
        )

    own_rows = pl.ds(pl.multiple_of(row * bs, bs), bs)

    def own_half(half):
        return feat_hbm.at[:, half * width:(half + 1) * width]

    block_load = load(0, blocks_hbm, blocks)
    col_load = load(1, col_hbm, cols)
    count_load = load(2, count_hbm, counts)
    own_loads = [load(5 + half, own_half(half), stripe.at[half, own_rows, :]) for half in range(HALVES)]
    weight_load = load(3, weight_hbm, weight)
    bias_load = load(4, bias_hbm, bias)

    def owner_of(i):
        down = n_out - 1 - i
        down = down - (down <= outer).astype(jnp.int32)
        up = i + (i >= outer).astype(jnp.int32)
        low = (outer < n_out // 2).astype(jnp.int32)
        last = jnp.where(i == n_out - 1, 1, 0)
        return last * outer + (1 - last) * (low * down + (1 - low) * up)

    pl.semaphore_wait(barrier, n_row - 1 + 1 + n_out - 1)

    gathers = []
    for half in range(HALVES):
        for shift in range(1, n_row):
            copy = pltpu.make_async_remote_copy(
                src_ref=own_half(half),
                dst_ref=stripe.at[half, own_rows, :],
                send_sem=ag_send.at[half, shift - 1],
                recv_sem=ag_recv.at[half, shift - 1],
                device_id=(lax.rem(row + shift, n_row), col),
                device_id_type=MESH,
            )
            copy.start()
            gathers.append(copy)

    col_load.wait()
    count_load.wait()
    block_load.wait()

    def build(slot, carry):
        group, i = slot // n_out, slot % n_out
        target = owner_of(i) * INNER + (1 - group) * (1 - inner) + group * inner
        rows = pl.ds(pl.multiple_of(slot * bs, bs), bs)
        count = counts[0, target]
        parts = [blocks[target, k].astype(jnp.float32) for k in range(slots)]
        for j in range(n_row):
            total = None
            for k in range(slots):
                live = jnp.logical_and(cols[k, target] == j, k < count)
                piece = parts[k] * jnp.where(live, 1.0, 0.0).astype(jnp.float32)
                total = piece if total is None else total + piece
            dense[rows, j * bs:(j + 1) * bs] = total.astype(jnp.bfloat16)
        return carry

    lax.fori_loop(0, INNER * n_out, build, 0)

    step = 4 if n_out % 4 == 0 else 1

    def multiply(half, group):
        def some(index, carry):
            first = group * n_out + index * step
            rows = pl.ds(pl.multiple_of(first * bs, bs), step * bs)
            value = jnp.dot(dense[rows, :], stripe[half], preferred_element_type=jnp.float32)
            terms[half, rows, :] = value.astype(jnp.bfloat16)
            return carry

        if n_out == step:
            some(0, 0)
        else:
            lax.fori_loop(0, n_out // step, some, 0)

    pairs = {}

    def send_pair(half, i):
        copy = pltpu.make_async_remote_copy(
            src_ref=terms.at[half, pl.ds(i * bs, bs), :],
            dst_ref=pair_in.at[half, i],
            send_sem=pair_send.at[half, i],
            recv_sem=pair_recv.at[half, i],
            device_id=(row, partner),
            device_id_type=MESH,
        )
        copy.start()
        pairs[half, i] = copy

    for half in range(HALVES):
        own_loads[half].wait()
        for shift in range(1, n_row):
            gathers[half * (n_row - 1) + shift - 1].wait_recv()
        multiply(half, 0)
        for i in range(n_out - 1):
            send_pair(half, i)
        if half == HALVES - 1:
            for other in range(HALVES):
                send_pair(other, n_out - 1)
        multiply(half, 1)

    def pair_sum(half, i):
        pairs[half, i].wait_recv()
        first = (n_out + i) * bs
        return terms[half, first:first + bs, :].astype(jnp.float32) + pair_in[half, i].astype(jnp.float32)

    owners = []
    for half in range(HALVES):
        for i in range(n_out - 1):
            pair_out[half, i] = pair_sum(half, i).astype(jnp.bfloat16)
            target = owner_of(i)
            shift = lax.rem(target - outer + n_out, n_out) - 1
            copy = pltpu.make_async_remote_copy(
                src_ref=pair_out.at[half, i],
                dst_ref=owner_in.at[half, shift],
                send_sem=owner_send.at[half, i],
                recv_sem=owner_recv.at[half, shift],
                device_id=(row, target * INNER + inner),
                device_id_type=MESH,
            )
            copy.start()
            owners.append(copy)
    mine = [pair_sum(half, n_out - 1) for half in range(HALVES)]

    bias_load.wait()
    weight_load.wait()
    hidden = bias[...]
    for half in range(HALVES):
        total = mine[half]
        for shift in range(n_out - 1):
            pltpu.make_async_remote_copy(
                src_ref=pair_out.at[half, 0],
                dst_ref=owner_in.at[half, shift],
                send_sem=owner_send.at[half, 0],
                recv_sem=owner_recv.at[half, shift],
                device_id=(row, partner),
                device_id_type=MESH,
            ).wait_recv()
            total = total + owner_in[half, shift].astype(jnp.float32)
        span = slice(half * width, (half + 1) * width)
        hidden = hidden + jnp.dot(total.astype(jnp.bfloat16), weight[span, :], preferred_element_type=jnp.float32)
    out_ref[...] = jnp.maximum(hidden, 0.0).astype(jnp.bfloat16)

    for copy in gathers + list(pairs.values()) + owners:
        copy.wait_send()


def local(n_row, n_col, features, blocks, block_col, row_count, weight, out_bias):
    bs, feat_width = blocks.shape[2], features.shape[1]
    n_out = n_col // INNER
    width = feat_width // HALVES
    bf16 = jnp.bfloat16
    return pl.pallas_call(
        functools.partial(layer_kernel, n_row, n_out, bs),
        out_shape=jax.ShapeDtypeStruct(features.shape, bf16),
        in_specs=[pl.BlockSpec(memory_space=pltpu.HBM)] * 6,
        out_specs=pl.BlockSpec(memory_space=pltpu.VMEM),
        scratch_shapes=[
            pltpu.VMEM(blocks.shape, bf16),
            pltpu.SMEM(block_col.shape[::-1], jnp.int32),
            pltpu.SMEM(row_count.shape[::-1], jnp.int32),
            pltpu.VMEM(weight.shape, bf16),
            pltpu.VMEM((1, feat_width), jnp.float32),
            pltpu.VMEM((HALVES, n_row * bs, width), bf16),
            pltpu.VMEM((n_col * bs, n_row * bs), bf16),
            pltpu.VMEM((HALVES, n_col * bs, width), bf16),
            pltpu.VMEM((HALVES, n_out, bs, width), bf16),
            pltpu.VMEM((HALVES, n_out - 1, bs, width), bf16),
            pltpu.VMEM((HALVES, n_out - 1, bs, width), bf16),
            pltpu.SemaphoreType.DMA((5 + HALVES,)),
            pltpu.SemaphoreType.DMA((HALVES, n_row - 1)),
            pltpu.SemaphoreType.DMA((HALVES, n_row - 1)),
            pltpu.SemaphoreType.DMA((HALVES, n_out)),
            pltpu.SemaphoreType.DMA((HALVES, n_out)),
            pltpu.SemaphoreType.DMA((HALVES, n_out - 1)),
            pltpu.SemaphoreType.DMA((HALVES, n_out - 1)),
        ],
        compiler_params=pltpu.CompilerParams(
            collective_id=0, has_side_effects=True, vmem_limit_bytes=58 * 1024 * 1024
        ),
    )(features, blocks, block_col.T, row_count.T, weight, out_bias.reshape(1, feat_width))


def solution(mesh):
    return jax.shard_map(
        functools.partial(local, mesh.shape["row"], mesh.shape["col"]),
        mesh=mesh,
        in_specs=(
            P(("row", "col"), None),
            P("row", "col", None, None),
            P("row", "col"),
            P("row", "col"),
            P(),
            P(),
        ),
        out_specs=P(("row", "col"), None),
        check_vma=False,
    )
```

```python
import functools

import jax
import jax.numpy as jnp
from jax import lax
from jax.experimental import pallas as pl
from jax.experimental.pallas import tpu as pltpu
from jax.sharding import PartitionSpec as P

MESH = pl.DeviceIdType.MESH
HALVES = 2
INNER = 2


def layer_kernel(
    n_row, n_out, bs,
    feat_hbm, blocks_hbm, col_hbm, count_hbm, weight_hbm, bias_hbm, out_ref,
    blocks, cols, counts, weight, bias, stripe, dense, terms, pair_in, pair_out, owner_in,
    load_sem, ag_send, ag_recv, pair_send, pair_recv, owner_send, owner_recv,
):
    row = lax.axis_index("row")
    col = lax.axis_index("col")
    outer, inner = col // INNER, col % INNER
    partner = outer * INNER + 1 - inner
    width = stripe.shape[2]
    slots = blocks.shape[1]

    def load(index, src, dst):
        copy = pltpu.make_async_copy(src, dst, load_sem.at[index])
        copy.start()
        return copy

    barrier = pltpu.get_barrier_semaphore()
    for shift in range(1, n_row):
        pl.semaphore_signal(barrier, inc=1, device_id=(lax.rem(row + shift, n_row), col), device_id_type=MESH)
    pl.semaphore_signal(barrier, inc=1, device_id=(row, partner), device_id_type=MESH)
    for shift in range(1, n_out):
        pl.semaphore_signal(
            barrier, inc=1, device_id=(row, lax.rem(outer + shift, n_out) * INNER + inner), device_id_type=MESH
        )

    def owner_of(i):
        down = n_out - 1 - i
        down = down - (down <= outer).astype(jnp.int32)
        up = i + (i >= outer).astype(jnp.int32)
        low = (outer < n_out // 2).astype(jnp.int32)
        last = jnp.where(i == n_out - 1, 1, 0)
        return last * outer + (1 - last) * (low * down + (1 - low) * up)

    own_rows = pl.ds(pl.multiple_of(row * bs, bs), bs)

    def own_half(half):
        return feat_hbm.at[:, half * width:(half + 1) * width]

    def target_of(group, i):
        return owner_of(i) * INNER + (inner if group else 1 - inner)

    col_load = load(0, col_hbm, cols)
    count_load = load(1, count_hbm, counts)
    block_loads = {}
    for group in range(INNER):
        for i in range(n_out):
            slot = group * n_out + i
            block_loads[group, i] = load(4 + HALVES + slot, blocks_hbm.at[target_of(group, i)], blocks.at[slot])
        if group == 0:
            own_loads = [load(4 + half, own_half(half), stripe.at[half, own_rows, :]) for half in range(HALVES)]
    weight_load = load(2, weight_hbm, weight)
    bias_load = load(3, bias_hbm, bias)


    pl.semaphore_wait(barrier, n_row - 1 + 1 + n_out - 1)

    gathers = []
    for half in range(HALVES):
        for shift in range(1, n_row):
            copy = pltpu.make_async_remote_copy(
                src_ref=own_half(half),
                dst_ref=stripe.at[half, own_rows, :],
                send_sem=ag_send.at[half, shift - 1],
                recv_sem=ag_recv.at[half, shift - 1],
                device_id=(lax.rem(row + shift, n_row), col),
                device_id_type=MESH,
            )
            copy.start()
            gathers.append(copy)

    col_load.wait()
    count_load.wait()

    def build(group):
        for i in range(n_out):
            block_loads[group, i].wait()
            slot, target = group * n_out + i, target_of(group, i)
            count = counts[0, target]
            live_cols = [jnp.where(k < count, cols[k, target], -1) for k in range(slots)]

            def column(j, carry):
                total = None
                for k in range(slots):
                    part = blocks[slot, k]
                    piece = jnp.where(live_cols[k] == j, part, jnp.zeros_like(part))
                    total = piece if total is None else total + piece
                dense[slot * bs:(slot + 1) * bs, pl.ds(pl.multiple_of(j * bs, bs), bs)] = total
                return carry

            if n_row <= 4:
                for j in range(n_row):
                    column(j, 0)
            else:
                lax.fori_loop(0, n_row, column, 0)

    build(0)
    step = 4 if n_out % 4 == 0 else 1

    def multiply(half, group):
        def some(index, carry):
            first = group * n_out + index * step
            rows = pl.ds(pl.multiple_of(first * bs, bs), step * bs)
            value = jnp.dot(dense[rows, :], stripe[half], preferred_element_type=jnp.float32)
            terms[half, rows, :] = value.astype(jnp.bfloat16)
            return carry

        if n_out == step:
            some(0, 0)
        else:
            lax.fori_loop(0, n_out // step, some, 0)

    pairs = {}

    def send_pair(half, i):
        copy = pltpu.make_async_remote_copy(
            src_ref=terms.at[half, pl.ds(i * bs, bs), :],
            dst_ref=pair_in.at[half, i],
            send_sem=pair_send.at[half, i],
            recv_sem=pair_recv.at[half, i],
            device_id=(row, partner),
            device_id_type=MESH,
        )
        copy.start()
        pairs[half, i] = copy

    def pair_sum(half, i):
        pairs[half, i].wait_recv()
        first = (n_out + i) * bs
        return terms[half, first:first + bs, :].astype(jnp.float32) + pair_in[half, i].astype(jnp.float32)

    owners = []

    def send_owner(half, i):
        pair_out[half, i] = pair_sum(half, i).astype(jnp.bfloat16)
        target = owner_of(i)
        shift = lax.rem(target - outer + n_out, n_out) - 1
        copy = pltpu.make_async_remote_copy(
            src_ref=pair_out.at[half, i],
            dst_ref=owner_in.at[half, shift],
            send_sem=owner_send.at[half, i],
            recv_sem=owner_recv.at[half, shift],
            device_id=(row, target * INNER + inner),
            device_id_type=MESH,
        )
        copy.start()
        owners.append(copy)

    for half in range(HALVES):
        own_loads[half].wait()
        for shift in range(1, n_row):
            gathers[half * (n_row - 1) + shift - 1].wait_recv()
        multiply(half, 0)
        for i in range(n_out - 1):
            send_pair(half, i)
        if half == 0:
            build(1)
            multiply(half, 1)
    for half in range(HALVES):
        send_pair(half, n_out - 1)
    for half in range(HALVES):
        if half:
            multiply(half, 1)
        for i in range(n_out - 1):
            send_owner(half, i)
    mine = [pair_sum(half, n_out - 1) for half in range(HALVES)]

    bias_load.wait()
    weight_load.wait()
    hidden = bias[...]
    for half in range(HALVES):
        total = mine[half]
        for shift in range(n_out - 1):
            pltpu.make_async_remote_copy(
                src_ref=pair_out.at[half, 0],
                dst_ref=owner_in.at[half, shift],
                send_sem=owner_send.at[half, 0],
                recv_sem=owner_recv.at[half, shift],
                device_id=(row, partner),
                device_id_type=MESH,
            ).wait_recv()
            total = total + owner_in[half, shift].astype(jnp.float32)
        span = slice(half * width, (half + 1) * width)
        hidden = hidden + jnp.dot(total.astype(jnp.bfloat16), weight[span, :], preferred_element_type=jnp.float32)
    out_ref[...] = jnp.maximum(hidden, 0.0).astype(jnp.bfloat16)

    for copy in gathers + list(pairs.values()) + owners:
        copy.wait_send()


def local(n_row, n_col, features, blocks, block_col, row_count, weight, out_bias):
    bs, feat_width = blocks.shape[2], features.shape[1]
    n_out = n_col // INNER
    width = feat_width // HALVES
    bf16 = jnp.bfloat16
    return pl.pallas_call(
        functools.partial(layer_kernel, n_row, n_out, bs),
        out_shape=jax.ShapeDtypeStruct(features.shape, bf16),
        in_specs=[pl.BlockSpec(memory_space=pltpu.HBM)] * 6,
        out_specs=pl.BlockSpec(memory_space=pltpu.VMEM),
        scratch_shapes=[
            pltpu.VMEM(blocks.shape, bf16),
            pltpu.SMEM(block_col.shape[::-1], jnp.int32),
            pltpu.SMEM(row_count.shape[::-1], jnp.int32),
            pltpu.VMEM(weight.shape, bf16),
            pltpu.VMEM((1, feat_width), jnp.float32),
            pltpu.VMEM((HALVES, n_row * bs, width), bf16),
            pltpu.VMEM((n_col * bs, n_row * bs), bf16),
            pltpu.VMEM((HALVES, n_col * bs, width), bf16),
            pltpu.VMEM((HALVES, n_out, bs, width), bf16),
            pltpu.VMEM((HALVES, n_out - 1, bs, width), bf16),
            pltpu.VMEM((HALVES, n_out - 1, bs, width), bf16),
            pltpu.SemaphoreType.DMA((4 + HALVES + n_col,)),
            pltpu.SemaphoreType.DMA((HALVES, n_row - 1)),
            pltpu.SemaphoreType.DMA((HALVES, n_row - 1)),
            pltpu.SemaphoreType.DMA((HALVES, n_out)),
            pltpu.SemaphoreType.DMA((HALVES, n_out)),
            pltpu.SemaphoreType.DMA((HALVES, n_out - 1)),
            pltpu.SemaphoreType.DMA((HALVES, n_out - 1)),
        ],
        compiler_params=pltpu.CompilerParams(
            collective_id=0, has_side_effects=True, vmem_limit_bytes=58 * 1024 * 1024
        ),
    )(features, blocks, block_col.T, row_count.T, weight, out_bias.reshape(1, feat_width))


def solution(mesh):
    return jax.shard_map(
        functools.partial(local, mesh.shape["row"], mesh.shape["col"]),
        mesh=mesh,
        in_specs=(
            P(("row", "col"), None),
            P("row", "col", None, None),
            P("row", "col"),
            P("row", "col"),
            P(),
            P(),
        ),
        out_specs=P(("row", "col"), None),
        check_vma=False,
    )
```

```python
import functools

import jax
import jax.numpy as jnp
from jax import lax
from jax.experimental import pallas as pl
from jax.experimental.pallas import tpu as pltpu
from jax.sharding import PartitionSpec as P

MESH = pl.DeviceIdType.MESH
HALVES = 2
INNER = 2


def layer_kernel(
    n_row, n_out, bs,
    feat_hbm, blocks_hbm, col_hbm, count_hbm, weight_hbm, bias_hbm, out_ref,
    blocks, cols, counts, weight, bias, stripe, dense, terms, pair_in, pair_out, owner_in,
    load_sem, ag_send, ag_recv, pair_send, pair_recv, owner_send, owner_recv,
):
    row = lax.axis_index("row")
    col = lax.axis_index("col")
    outer, inner = col // INNER, col % INNER
    partner = outer * INNER + 1 - inner
    width = stripe.shape[2]
    slots = blocks.shape[1]

    def load(index, src, dst):
        copy = pltpu.make_async_copy(src, dst, load_sem.at[index])
        copy.start()
        return copy

    barrier = pltpu.get_barrier_semaphore()
    for shift in range(1, n_row):
        pl.semaphore_signal(barrier, inc=1, device_id=(lax.rem(row + shift, n_row), col), device_id_type=MESH)
    pl.semaphore_signal(barrier, inc=1, device_id=(row, partner), device_id_type=MESH)
    for shift in range(1, n_out):
        pl.semaphore_signal(
            barrier, inc=1, device_id=(row, lax.rem(outer + shift, n_out) * INNER + inner), device_id_type=MESH
        )

    def owner_of(i):
        down = n_out - 1 - i
        down = down - (down <= outer).astype(jnp.int32)
        up = i + (i >= outer).astype(jnp.int32)
        low = (outer < n_out // 2).astype(jnp.int32)
        last = jnp.where(i == n_out - 1, 1, 0)
        return last * outer + (1 - last) * (low * down + (1 - low) * up)

    own_rows = pl.ds(pl.multiple_of(row * bs, bs), bs)

    def own_half(half):
        return feat_hbm.at[:, half * width:(half + 1) * width]

    def target_of(group, i):
        return owner_of(i) * INNER + (inner if group else 1 - inner)

    col_load = load(0, col_hbm, cols)
    count_load = load(1, count_hbm, counts)
    block_loads = {}
    for group in range(INNER):
        for i in range(n_out):
            slot = group * n_out + i
            block_loads[group, i] = load(4 + HALVES + slot, blocks_hbm.at[target_of(group, i)], blocks.at[slot])
        if group == 0:
            own_loads = [load(4 + half, own_half(half), stripe.at[half, own_rows, :]) for half in range(HALVES)]
    weight_load = load(2, weight_hbm, weight)
    bias_load = load(3, bias_hbm, bias)


    pl.semaphore_wait(barrier, n_row - 1 + 1 + n_out - 1)

    gathers = []
    for half in range(HALVES):
        for shift in range(1, n_row):
            copy = pltpu.make_async_remote_copy(
                src_ref=own_half(half),
                dst_ref=stripe.at[half, own_rows, :],
                send_sem=ag_send.at[half, shift - 1],
                recv_sem=ag_recv.at[half, shift - 1],
                device_id=(lax.rem(row + shift, n_row), col),
                device_id_type=MESH,
            )
            copy.start()
            gathers.append(copy)

    col_load.wait()
    count_load.wait()

    def build(group):
        for i in range(n_out):
            block_loads[group, i].wait()
            slot, target = group * n_out + i, target_of(group, i)
            count = counts[0, target]
            live_cols = [jnp.where(k < count, cols[k, target], -1) for k in range(slots)]

            def column(j, carry):
                total = None
                for k in range(slots):
                    part = blocks[slot, k]
                    piece = jnp.where(live_cols[k] == j, part, jnp.zeros_like(part))
                    total = piece if total is None else total + piece
                dense[slot * bs:(slot + 1) * bs, pl.ds(pl.multiple_of(j * bs, bs), bs)] = total
                return carry

            if n_row <= 4:
                for j in range(n_row):
                    column(j, 0)
            else:
                lax.fori_loop(0, n_row, column, 0)

    build(0)
    step = 4 if n_out % 4 == 0 else 1

    def multiply(half, group):
        def some(index, carry):
            first = group * n_out + index * step
            rows = pl.ds(pl.multiple_of(first * bs, bs), step * bs)
            value = jnp.dot(dense[rows, :], stripe[half], preferred_element_type=jnp.float32)
            terms[half, rows, :] = value.astype(jnp.bfloat16)
            return carry

        if n_out == step:
            some(0, 0)
        else:
            lax.fori_loop(0, n_out // step, some, 0)

    pairs = {}

    def send_pair(half, i):
        copy = pltpu.make_async_remote_copy(
            src_ref=terms.at[half, pl.ds(i * bs, bs), :],
            dst_ref=pair_in.at[half, i],
            send_sem=pair_send.at[half, i],
            recv_sem=pair_recv.at[half, i],
            device_id=(row, partner),
            device_id_type=MESH,
        )
        copy.start()
        pairs[half, i] = copy

    def pair_sum(half, i):
        pairs[half, i].wait_recv()
        first = (n_out + i) * bs
        return terms[half, first:first + bs, :].astype(jnp.float32) + pair_in[half, i].astype(jnp.float32)

    owners = []

    def send_owner(half, i):
        pair_out[half, i] = pair_sum(half, i).astype(jnp.bfloat16)
        target = owner_of(i)
        shift = lax.rem(target - outer + n_out, n_out) - 1
        copy = pltpu.make_async_remote_copy(
            src_ref=pair_out.at[half, i],
            dst_ref=owner_in.at[half, shift],
            send_sem=owner_send.at[half, i],
            recv_sem=owner_recv.at[half, shift],
            device_id=(row, target * INNER + inner),
            device_id_type=MESH,
        )
        copy.start()
        owners.append(copy)

    for half in range(HALVES):
        own_loads[half].wait()
        for shift in range(1, n_row):
            gathers[half * (n_row - 1) + shift - 1].wait_recv()
        multiply(half, 0)
        for i in range(n_out - 1):
            send_pair(half, i)
        if half == 0:
            build(1)
            multiply(half, 1)
    for half in range(HALVES):
        send_pair(half, n_out - 1)
    for half in range(HALVES):
        if half:
            multiply(half, 1)
        for i in range(n_out - 1):
            send_owner(half, i)
    mine = [pair_sum(half, n_out - 1) for half in range(HALVES)]

    bias_load.wait()
    weight_load.wait()
    hidden = bias[...]
    for half in range(HALVES):
        total = mine[half]
        for shift in range(n_out - 1):
            pltpu.make_async_remote_copy(
                src_ref=pair_out.at[half, 0],
                dst_ref=owner_in.at[half, shift],
                send_sem=owner_send.at[half, 0],
                recv_sem=owner_recv.at[half, shift],
                device_id=(row, partner),
                device_id_type=MESH,
            ).wait_recv()
            total = total + owner_in[half, shift].astype(jnp.float32)
        span = slice(half * width, (half + 1) * width)
        hidden = hidden + jnp.dot(total.astype(jnp.bfloat16), weight[span, :], preferred_element_type=jnp.float32)
    out_ref[...] = jnp.maximum(hidden, 0.0).astype(jnp.bfloat16)

    for copy in gathers + list(pairs.values()) + owners:
        copy.wait_send()


def local(n_row, n_col, features, blocks, block_col, row_count, weight, out_bias):
    bs, feat_width = blocks.shape[2], features.shape[1]
    n_out = n_col // INNER
    width = feat_width // HALVES
    bf16 = jnp.bfloat16
    return pl.pallas_call(
        functools.partial(layer_kernel, n_row, n_out, bs),
        out_shape=pltpu.VMEM(features.shape, bf16),
        in_specs=[pl.BlockSpec(memory_space=pltpu.HBM)] * 6,
        out_specs=pl.BlockSpec(memory_space=pltpu.VMEM),
        scratch_shapes=[
            pltpu.VMEM(blocks.shape, bf16),
            pltpu.SMEM(block_col.shape[::-1], jnp.int32),
            pltpu.SMEM(row_count.shape[::-1], jnp.int32),
            pltpu.VMEM(weight.shape, bf16),
            pltpu.VMEM((1, feat_width), jnp.float32),
            pltpu.VMEM((HALVES, n_row * bs, width), bf16),
            pltpu.VMEM((n_col * bs, n_row * bs), bf16),
            pltpu.VMEM((HALVES, n_col * bs, width), bf16),
            pltpu.VMEM((HALVES, n_out, bs, width), bf16),
            pltpu.VMEM((HALVES, n_out - 1, bs, width), bf16),
            pltpu.VMEM((HALVES, n_out - 1, bs, width), bf16),
            pltpu.SemaphoreType.DMA((4 + HALVES + n_col,)),
            pltpu.SemaphoreType.DMA((HALVES, n_row - 1)),
            pltpu.SemaphoreType.DMA((HALVES, n_row - 1)),
            pltpu.SemaphoreType.DMA((HALVES, n_out)),
            pltpu.SemaphoreType.DMA((HALVES, n_out)),
            pltpu.SemaphoreType.DMA((HALVES, n_out - 1)),
            pltpu.SemaphoreType.DMA((HALVES, n_out - 1)),
        ],
        compiler_params=pltpu.CompilerParams(
            collective_id=0, has_side_effects=True, vmem_limit_bytes=58 * 1024 * 1024
        ),
    )(features, blocks, block_col.T, row_count.T, weight, out_bias.reshape(1, feat_width))


def solution(mesh):
    return jax.shard_map(
        functools.partial(local, mesh.shape["row"], mesh.shape["col"]),
        mesh=mesh,
        in_specs=(
            P(("row", "col"), None),
            P("row", "col", None, None),
            P("row", "col"),
            P("row", "col"),
            P(),
            P(),
        ),
        out_specs=P(("row", "col"), None),
        check_vma=False,
    )
```

```python
import functools

import jax
import jax.numpy as jnp
from jax import lax
from jax.experimental import pallas as pl
from jax.experimental.pallas import tpu as pltpu
from jax.sharding import PartitionSpec as P

MESH = pl.DeviceIdType.MESH
HALVES = 2
INNER = 2


def layer_kernel(
    n_row, n_out, bs,
    feat_hbm, blocks_hbm, col_hbm, count_hbm, weight_hbm, bias_hbm, out_ref,
    blocks, cols, counts, weight, bias, stripe, dense, terms, pair_in, pair_out, owner_in,
    load_sem, ag_send, ag_recv, pair_send, pair_recv, owner_send, owner_recv,
):
    row = lax.axis_index("row")
    col = lax.axis_index("col")
    outer, inner = col // INNER, col % INNER
    partner = outer * INNER + 1 - inner
    width = stripe.shape[2]
    slots = blocks.shape[1]

    def load(index, src, dst):
        copy = pltpu.make_async_copy(src, dst, load_sem.at[index])
        copy.start()
        return copy

    barrier = pltpu.get_barrier_semaphore()
    for shift in range(1, n_row):
        pl.semaphore_signal(barrier, inc=1, device_id=(lax.rem(row + shift, n_row), col), device_id_type=MESH)
    pl.semaphore_signal(barrier, inc=1, device_id=(row, partner), device_id_type=MESH)
    for shift in range(1, n_out):
        pl.semaphore_signal(
            barrier, inc=1, device_id=(row, lax.rem(outer + shift, n_out) * INNER + inner), device_id_type=MESH
        )

    def owner_of(i):
        down = n_out - 1 - i
        down = down - (down <= outer).astype(jnp.int32)
        up = i + (i >= outer).astype(jnp.int32)
        low = (outer < n_out // 2).astype(jnp.int32)
        last = jnp.where(i == n_out - 1, 1, 0)
        return last * outer + (1 - last) * (low * down + (1 - low) * up)

    own_rows = pl.ds(pl.multiple_of(row * bs, bs), bs)

    def own_half(half):
        return feat_hbm.at[:, half * width:(half + 1) * width]

    def target_of(group, i):
        return owner_of(i) * INNER + (inner if group else 1 - inner)

    col_load = load(0, col_hbm, cols)
    count_load = load(1, count_hbm, counts)
    block_loads = {}
    for group in range(INNER):
        for i in range(n_out):
            slot = group * n_out + i
            block_loads[group, i] = load(4 + HALVES + slot, blocks_hbm.at[target_of(group, i)], blocks.at[slot])
        if group == 0:
            own_loads = [load(4 + half, own_half(half), stripe.at[half, own_rows, :]) for half in range(HALVES)]
    weight_load = load(2, weight_hbm, weight)
    bias_load = load(3, bias_hbm, bias)


    pl.semaphore_wait(barrier, n_row - 1 + 1 + n_out - 1)

    gathers = []
    for half in range(HALVES):
        for shift in range(1, n_row):
            copy = pltpu.make_async_remote_copy(
                src_ref=own_half(half),
                dst_ref=stripe.at[half, own_rows, :],
                send_sem=ag_send.at[half, shift - 1],
                recv_sem=ag_recv.at[half, shift - 1],
                device_id=(lax.rem(row + shift, n_row), col),
                device_id_type=MESH,
            )
            copy.start()
            gathers.append(copy)

    col_load.wait()
    count_load.wait()

    def build(group):
        for i in range(n_out):
            block_loads[group, i].wait()
            slot, target = group * n_out + i, target_of(group, i)
            count = counts[0, target]
            live_cols = [jnp.where(k < count, cols[k, target], -1) for k in range(slots)]

            def column(j, carry):
                total = None
                for k in range(slots):
                    part = blocks[slot, k]
                    piece = jnp.where(live_cols[k] == j, part, jnp.zeros_like(part))
                    total = piece if total is None else total + piece
                dense[slot * bs:(slot + 1) * bs, pl.ds(pl.multiple_of(j * bs, bs), bs)] = total
                return carry

            if n_row <= 4:
                for j in range(n_row):
                    column(j, 0)
            else:
                lax.fori_loop(0, n_row, column, 0)

    build(0)
    step = 4 if n_out % 4 == 0 else 1

    def multiply(half, group):
        def some(index, carry):
            first = group * n_out + index * step
            rows = pl.ds(pl.multiple_of(first * bs, bs), step * bs)
            value = jnp.dot(dense[rows, :], stripe[half], preferred_element_type=jnp.float32)
            terms[half, rows, :] = value.astype(jnp.bfloat16)
            return carry

        if n_out == step:
            some(0, 0)
        else:
            lax.fori_loop(0, n_out // step, some, 0)

    pairs = {}

    def send_pair(half, i):
        copy = pltpu.make_async_remote_copy(
            src_ref=terms.at[half, pl.ds(i * bs, bs), :],
            dst_ref=pair_in.at[half, i],
            send_sem=pair_send.at[half, i],
            recv_sem=pair_recv.at[half, i],
            device_id=(row, partner),
            device_id_type=MESH,
        )
        copy.start()
        pairs[half, i] = copy

    def pair_sum(half, i):
        pairs[half, i].wait_recv()
        first = (n_out + i) * bs
        return terms[half, first:first + bs, :].astype(jnp.float32) + pair_in[half, i].astype(jnp.float32)

    owners = []

    def send_owner(half, i):
        pair_out[half, i] = pair_sum(half, i).astype(jnp.bfloat16)
        target = owner_of(i)
        shift = lax.rem(target - outer + n_out, n_out) - 1
        copy = pltpu.make_async_remote_copy(
            src_ref=pair_out.at[half, i],
            dst_ref=owner_in.at[half, shift],
            send_sem=owner_send.at[half, i],
            recv_sem=owner_recv.at[half, shift],
            device_id=(row, target * INNER + inner),
            device_id_type=MESH,
        )
        copy.start()
        owners.append(copy)

    for half in range(HALVES):
        own_loads[half].wait()
        for shift in range(1, n_row):
            gathers[half * (n_row - 1) + shift - 1].wait_recv()
        for first in range(0, n_out, INNER):
            rows = slice(first * bs, (first + INNER) * bs)
            value = jnp.dot(dense[rows, :], stripe[half], preferred_element_type=jnp.float32)
            terms[half, rows, :] = value.astype(jnp.bfloat16)
            for i in range(first, min(first + INNER, n_out - 1)):
                send_pair(half, i)
        if half == 0:
            build(1)
            multiply(half, 1)
    for half in range(HALVES):
        send_pair(half, n_out - 1)
    for half in range(HALVES):
        if half:
            multiply(half, 1)
        for i in range(n_out - 1):
            send_owner(half, i)
    mine = [pair_sum(half, n_out - 1) for half in range(HALVES)]

    bias_load.wait()
    weight_load.wait()
    hidden = bias[...]
    for half in range(HALVES):
        total = mine[half]
        for shift in range(n_out - 1):
            pltpu.make_async_remote_copy(
                src_ref=pair_out.at[half, 0],
                dst_ref=owner_in.at[half, shift],
                send_sem=owner_send.at[half, 0],
                recv_sem=owner_recv.at[half, shift],
                device_id=(row, partner),
                device_id_type=MESH,
            ).wait_recv()
            total = total + owner_in[half, shift].astype(jnp.float32)
        span = slice(half * width, (half + 1) * width)
        hidden = hidden + jnp.dot(total.astype(jnp.bfloat16), weight[span, :], preferred_element_type=jnp.float32)
    out_ref[...] = jnp.maximum(hidden, 0.0).astype(jnp.bfloat16)

    for copy in gathers + list(pairs.values()) + owners:
        copy.wait_send()


def local(n_row, n_col, features, blocks, block_col, row_count, weight, out_bias):
    bs, feat_width = blocks.shape[2], features.shape[1]
    n_out = n_col // INNER
    width = feat_width // HALVES
    bf16 = jnp.bfloat16
    return pl.pallas_call(
        functools.partial(layer_kernel, n_row, n_out, bs),
        out_shape=pltpu.VMEM(features.shape, bf16),
        in_specs=[pl.BlockSpec(memory_space=pltpu.HBM)] * 6,
        out_specs=pl.BlockSpec(memory_space=pltpu.VMEM),
        scratch_shapes=[
            pltpu.VMEM(blocks.shape, bf16),
            pltpu.SMEM(block_col.shape[::-1], jnp.int32),
            pltpu.SMEM(row_count.shape[::-1], jnp.int32),
            pltpu.VMEM(weight.shape, bf16),
            pltpu.VMEM((1, feat_width), jnp.float32),
            pltpu.VMEM((HALVES, n_row * bs, width), bf16),
            pltpu.VMEM((n_col * bs, n_row * bs), bf16),
            pltpu.VMEM((HALVES, n_col * bs, width), bf16),
            pltpu.VMEM((HALVES, n_out, bs, width), bf16),
            pltpu.VMEM((HALVES, n_out - 1, bs, width), bf16),
            pltpu.VMEM((HALVES, n_out - 1, bs, width), bf16),
            pltpu.SemaphoreType.DMA((4 + HALVES + n_col,)),
            pltpu.SemaphoreType.DMA((HALVES, n_row - 1)),
            pltpu.SemaphoreType.DMA((HALVES, n_row - 1)),
            pltpu.SemaphoreType.DMA((HALVES, n_out)),
            pltpu.SemaphoreType.DMA((HALVES, n_out)),
            pltpu.SemaphoreType.DMA((HALVES, n_out - 1)),
            pltpu.SemaphoreType.DMA((HALVES, n_out - 1)),
        ],
        compiler_params=pltpu.CompilerParams(
            collective_id=0, has_side_effects=True, vmem_limit_bytes=58 * 1024 * 1024
        ),
    )(features, blocks, block_col.T, row_count.T, weight, out_bias.reshape(1, feat_width))


def solution(mesh):
    return jax.shard_map(
        functools.partial(local, mesh.shape["row"], mesh.shape["col"]),
        mesh=mesh,
        in_specs=(
            P(("row", "col"), None),
            P("row", "col", None, None),
            P("row", "col"),
            P("row", "col"),
            P(),
            P(),
        ),
        out_specs=P(("row", "col"), None),
        check_vma=False,
    )
```
